32 devices in a mesh: dp: 4 (over y, core), mp: 8 (over z, x).
Axes of the slice: x: 2, y: 2, z: 4, core: 2. Of those that a mesh axis runs over, the one named last changes fastest.
Arguments:
- tokens: bfloat16 [16384, 1152], P(('dp', 'mp')), may hold values from -6 to 6
- conditioning: bfloat16 [64, 1152], P('dp'), may hold values from -6 to 6
- counts: int32 [4], P('dp'), may hold values from 1 to 16, as said below
- offset_index: int32 [256, 256], replicated, may hold values from 0 to 960, as said below
- modulator: bfloat16 [1152, 6912], P(None, 'mp'), may hold values from -0.1875 to 0.1875
- modulator_bias: bfloat16 [6912], P('mp'), may hold values from -3 to 3
- qkv_weight: bfloat16 [1152, 3, 1152], P(None, None, 'mp'), may hold values from -0.1875 to 0.1875
- qv_bias: bfloat16 [2, 1152], P(None, 'mp'), may hold values from -3 to 3
- offset_table: bfloat16 [961, 16], P(None, 'mp'), may hold values from -4 to 4
- out_weight: bfloat16 [1152, 1152], P('mp'), may hold values from -1 to 1
- out_bias: bfloat16 [1152], replicated, may hold values from -3 to 3
- up_weight: bfloat16 [1152, 4608], P(None, 'mp'), may hold values from -0.1875 to 0.1875
- up_bias: bfloat16 [4608], P('mp'), may hold values from -3 to 3
- down_weight: bfloat16 [4608, 1152], P('mp'), may hold values from -0.09375 to 0.09375
- down_bias: bfloat16 [1152], replicated, may hold values from -3 to 3
- out_grad: bfloat16 [16384, 1152], P(('dp', 'mp')), may hold values from -6 to 6
Outputs:
- block_out: bfloat16 [16384, 1152], P(('dp', 'mp'))
- tokens_grad: float32 [16384, 1152], P(('dp', 'mp'))
- cond_grad: float32 [64, 1152], P('dp')
- modulator_grad: float32 [1152, 6912], P(None, 'mp')
- modulator_bias_grad: float32 [6912], P('mp')
- qkv_grad: float32 [1152, 3, 1152], P(None, None, 'mp')
- qv_bias_grad: float32 [2, 1152], P(None, 'mp')
- offset_table_grad: float32 [961, 16], P(None, 'mp')
- out_weight_grad: float32 [1152, 1152], P('mp')
- out_bias_grad: float32 [1152], replicated
- up_grad: float32 [1152, 4608], P(None, 'mp')
- up_bias_grad: float32 [4608], P('mp')
- down_grad: float32 [4608, 1152], P('mp')
- down_bias_grad: float32 [1152], replicated
The draws below stay inside these ranges and needn't reach their ends.
Inputs may be any that keep to these rules, and one draw needn't show every extreme that they name: counts[g] is how many of the 16 sample slots of index g of dp hold a live sample (the first ones); at least one index holds 16. offset_index[i, j] depends only on the displacement between patches i and j on the 16 x 16 grid (patch p at row p // 16, column p mod 16); distinct displacements have distinct entries.
All inputs are finite; a program needn't handle non-finite values.
Results may differ from the reference program's by a relative error of at most 0.02.
The reference program's roundings to bfloat16 on the way count: a program that leaves them out, or rounds other values in their place, can miss the bound.
Values may be sent and summed in bfloat16 or wider, within the bound.
No kernel may reach another device: no remote copies, remote signals or barrier semaphores. Data moves between devices by JAX's collectives and lax.ppermute only.
A program may use at most 256 MiB of HBM per device.

```python
import math
from functools import partial
import jax
import jax.numpy as jnp
from jax import lax

D = 1152
HEADS = 16
FF = 4608
GRID = 16
SAMP_DEV = 16
HS = 72
PATCHES = 256
REL = 961
SAMPLES = 64
TOKENS = 16384
N_DP = 4


def draw_counts(key, part):
    base = jax.random.randint(jax.random.fold_in(key, 11), (N_DP,), 1, SAMP_DEV + 1)
    fullest = jax.random.randint(jax.random.fold_in(key, 12), (), 0, N_DP)
    return jnp.where(jnp.arange(N_DP) == fullest, SAMP_DEV, base).astype(jnp.int32)


def draw_offset_index(key, part):
    positions = jnp.arange(PATCHES, dtype=jnp.int32)
    grid_rows = positions // GRID
    grid_cols = positions % GRID
    stride_width = 2 * GRID - 1
    canonical = (grid_rows[:, None] - grid_rows[None, :] + GRID - 1) * stride_width + (grid_cols[:, None] - grid_cols[None, :] + GRID - 1)
    relabel = jax.random.permutation(jax.random.fold_in(key, 13), REL).astype(jnp.int32)
    return relabel[canonical]


def block_scale(key, extent, cuts, smallest, top_value):
    def one(axis_at, parts):
        heights = jax.random.uniform(jax.random.fold_in(jax.random.fold_in(key, 6), axis_at), (parts,), jnp.float32, smallest / len(cuts), top_value / len(cuts))
        return jnp.repeat(jnp.exp(heights), extent[axis_at] // parts).reshape((-1,) + (1,) * (len(extent) - axis_at - 1))

    gain = one(*cuts[0])
    for cut in cuts[1:]:
        gain = gain * one(*cut)
    return gain


def noise(rng, shape, width, limit, cuts=(), kind=jnp.bfloat16):
    values = jax.random.normal(rng, shape, jnp.float32) * width
    if len(cuts) > 0:
        values = block_scale(rng, shape, cuts, -0.22, 0.18) * values
    return jnp.clip(values, min=-limit, max=limit).astype(kind)


def setup_inputs(seed: int = 0) -> dict:
    splits = jax.random.split(jax.random.key(seed), 17)
    tokens = noise(splits[0], (TOKENS, D), 1.0, 6.0, ((0, 32),))
    conditioning = noise(splits[1], (SAMPLES, D), 1.0, 6.0, ((0, 4),))
    counts = draw_counts(jax.random.fold_in(splits[16], 71), 0)
    offset_index = draw_offset_index(jax.random.fold_in(splits[16], 71), 0)
    modulator = noise(splits[4], (D, 6 * D), D ** -0.5, 0.1875, ((1, 8),))
    modulator_bias = noise(splits[5], (6 * D,), 0.5, 3.0, ((0, 8),))
    qkv_weight = noise(splits[6], (D, 3, D), D ** -0.5, 0.1875, ((2, 8),))
    qv_bias = noise(splits[7], (2, D), 0.5, 3.0, ((1, 8),))
    offset_table = noise(splits[8], (REL, HEADS), 1.0, 4.0, ((1, 8),))
    out_weight = noise(splits[9], (D, D), (D // 32) ** -0.5, 1.0, ((0, 8),))
    out_bias = noise(splits[10], (D,), 0.5, 3.0)
    up_weight = noise(splits[11], (D, FF), D ** -0.5, 0.1875, ((1, 8),))
    up_bias = noise(splits[12], (FF,), 0.5, 3.0, ((0, 8),))
    down_weight = noise(splits[13], (FF, D), FF ** -0.5, 0.09375, ((0, 8),))
    down_bias = noise(splits[14], (D,), 0.5, 3.0)
    out_grad = noise(splits[15], (TOKENS, D), 1.0, 6.0, ((0, 32),))
    return dict(tokens=tokens, conditioning=conditioning, counts=counts, offset_index=offset_index, modulator=modulator, modulator_bias=modulator_bias, qkv_weight=qkv_weight, qv_bias=qv_bias, offset_table=offset_table, out_weight=out_weight, out_bias=out_bias, up_weight=up_weight, up_bias=up_bias, down_weight=down_weight, down_bias=down_bias, out_grad=out_grad)


HIGHEST = lax.Precision.HIGHEST
EPSILON = 1e-06

@jax.custom_vjp
def low(v):
    return lax.optimization_barrier(v.astype(jnp.bfloat16)).astype(jnp.float32)

@jax.custom_vjp
def low_back(v):
    return v

def low_keep(v):
    return (low(v), None)

def low_pass(kept, grad):
    return (grad,)

def back_keep(v):
    return (v, None)

def back_low(kept, grad):
    return (low(grad),)
low.defvjp(low_keep, low_pass)
low_back.defvjp(back_keep, back_low)

def normalize(values):
    centred = values - lax.optimization_barrier(jnp.mean(values, axis=-1, keepdims=True))
    return centred * lax.rsqrt(lax.optimization_barrier(jnp.mean(centred * centred, axis=-1, keepdims=True)) + EPSILON)

def block_fn(weights, block_tokens, block_mod, block_live, offset_index):
    qkv_weight, qv_bias, offset_table, out_weight, out_bias, up_weight, up_bias, down_weight, down_bias = weights
    group = block_tokens.shape[0]
    blocks_six = [block_mod[:, None, number * D:(number + 1) * D] for number in range(6)]
    shift_one, scale_one, gate_one, shift_two, scale_two, gate_two = blocks_six
    input_one = low(normalize(block_tokens) * (1.0 + scale_one) + shift_one)
    projected = jnp.einsum('spd,dce->spce', input_one, qkv_weight, precision=HIGHEST)
    qkv_bias = jnp.stack([qv_bias[0], jnp.zeros_like(qv_bias[0]), qv_bias[1]])
    projected = low(low_back(projected + qkv_bias))
    projected = projected.reshape(group, PATCHES, 3, HEADS, HS)
    query_block = projected[:, :, 0]
    key_block = projected[:, :, 1]
    value_block = projected[:, :, 2]
    position_bias = jnp.transpose(offset_table[offset_index], (2, 0, 1))
    scores = jnp.einsum('sqhe,skhe->shqk', query_block, key_block, precision=HIGHEST) * HS ** (-0.5)
    scores = low_back(scores + position_bias[None])
    soft_weights = low(jax.nn.softmax(scores, axis=-1))
    attended = jnp.einsum('shqk,skhe->sqhe', soft_weights, value_block, precision=HIGHEST)
    attended = low(low_back(attended.reshape(group, PATCHES, D)))
    attn_branch = low_back(jnp.einsum('spd,de->spe', attended, out_weight, precision=HIGHEST) + out_bias)
    mid_tokens = block_tokens + gate_one * attn_branch
    input_two = low(normalize(mid_tokens) * (1.0 + scale_two) + shift_two)
    pre_act = low_back(jnp.einsum('spd,df->spf', input_two, up_weight, precision=HIGHEST) + up_bias)
    hidden = low(jax.nn.gelu(pre_act, approximate=True))
    mlp_branch = low_back(jnp.einsum('spf,fd->spd', hidden, down_weight, precision=HIGHEST) + down_bias)
    final_rows = mid_tokens + gate_two * mlp_branch
    return final_rows * block_live[:, None, None]

def forward(offset_index, live, tokens, conditioning, modulator, modulator_bias, qkv_weight, qv_bias, offset_table, out_weight, out_bias, up_weight, up_bias, down_weight, down_bias):
    activated = low(jax.nn.silu(conditioning))
    modulation = low_back(jnp.dot(activated, modulator, precision=HIGHEST) + modulator_bias)
    samples = conditioning.shape[0]
    group = math.gcd(samples, 16)
    blocks = samples // group
    weights = (qkv_weight, qv_bias, offset_table, out_weight, out_bias, up_weight, up_bias, down_weight, down_bias)
    stepper = jax.checkpoint(partial(block_fn, offset_index=offset_index))

    def map_step(inputs):
        return stepper(weights, inputs[0], inputs[1], inputs[2])
    results = lax.map(map_step, (tokens.reshape(blocks, group, PATCHES, D), modulation.reshape(blocks, group, 6 * D), live.reshape(blocks, group)))
    return results.reshape(samples * PATCHES, D)

def reference(tokens, conditioning, counts, offset_index, modulator, modulator_bias, qkv_weight, qv_bias, offset_table, out_weight, out_bias, up_weight, up_bias, down_weight, down_bias, out_grad):
    samples = conditioning.shape[0]
    sample_ids = jnp.arange(samples, dtype=jnp.int32)
    live = (sample_ids % SAMP_DEV < counts[sample_ids // SAMP_DEV]).astype(jnp.float32)
    floats = [value.astype(jnp.float32) for value in (tokens, conditioning, modulator, modulator_bias, qkv_weight, qv_bias, offset_table, out_weight, out_bias, up_weight, up_bias, down_weight, down_bias)]
    block_out, pullback = jax.vjp(partial(forward, offset_index, live), *floats)
    grads = pullback(out_grad.astype(jnp.float32))
    return (block_out.astype(jnp.bfloat16), grads[0], grads[1], grads[2], grads[3], grads[4], grads[5], grads[6], grads[7], grads[8], grads[9], grads[10], grads[11], grads[12])
```

```python
from functools import partial

import jax
import jax.numpy as jnp
from jax import lax
from jax.experimental import pallas as pl
from jax.experimental.pallas import tpu as pltpu
from jax.sharding import PartitionSpec as P

HS = 72
EPSILON = 1e-06
HIGHEST = lax.Precision.HIGHEST
BOTH = ("dp", "mp")
VMEM_BYTES = 44 * 2**20
BF16 = jnp.bfloat16
F32 = jnp.float32


def low(value):
    return value.astype(BF16)


def low_sum(*values):
    total = values[0].astype(F32)
    for value in values[1:]:
        total = total + value.astype(F32)
    return low(total)


class PairPlan:
    def __init__(self, mesh):
        self.zs = mesh.shape["mp"] // 2
        zs = self.zs
        self.core = self.moves(lambda y, c, z, x: (y, 1 - c, z, x))
        self.across_x = self.moves(lambda y, c, z, x: (y, c, z, 1 - x))
        self.across_y = self.moves(lambda y, c, z, x: (1 - y, c, z, x))
        self.up = self.moves(lambda y, c, z, x: (y, c, (z + 1) % zs, x))
        self.down = self.moves(lambda y, c, z, x: (y, c, (z - 1) % zs, x))

    def moves(self, target):
        def number(y, c, z, x):
            return ((y * 2 + c) * self.zs + z) * 2 + x

        places = [(y, c, z, x) for y in (0, 1) for c in (0, 1) for z in range(self.zs) for x in (0, 1)]
        return [(number(*place), number(*target(*place))) for place in places]

    def here(self):
        dp, mp = lax.axis_index("dp"), lax.axis_index("mp")
        return dp // 2, dp % 2, mp // 2, mp % 2

    def first_half(self):
        return self.here()[0]

    def move(self, value, way):
        return lax.ppermute(value, BOTH, way)

    def turned(self, values, halves):
        y, c, z, x = self.here()
        places = jnp.arange(self.zs)
        pick = (places[:, None] + places[None, :]) % self.zs == z
        pick = pick.reshape(pick.shape + (1,) * (values.ndim - 1))
        values = jnp.sum(jnp.where(pick, values[None], jnp.zeros_like(values[None])), axis=1)
        values = jnp.where(x == 0, values, values[:, ::-1])
        values = jnp.where(c == 0, values, values[:, :, ::-1])
        if halves:
            values = jnp.where(y == 0, values, values[:, :, :, ::-1])
        return values

    def to_own(self, values, halves):
        rest = values.shape[1:]
        lead = (self.zs, 2, 2, 2) if halves else (self.zs, 2, 2)
        split = values.reshape(lead + (-1,) + rest)
        split = self.turned(split, halves)
        split = split.transpose((2, 1, 0) + tuple(range(3, split.ndim)))
        return split.reshape((2, values.shape[0] // 2) + rest)

    def to_whole(self, values, halves):
        rest = values.shape[2:]
        lead = (2, 2, self.zs, 2) if halves else (2, 2, self.zs)
        split = values.reshape(lead + (-1,) + rest)
        split = split.transpose((2, 1, 0) + tuple(range(3, split.ndim)))
        return self.turned(split, halves).reshape((-1,) + rest)

    def gather(self, shard, light):
        y, c, _, _ = self.here()
        rows, width = shard.shape
        shard = shard.reshape(2, 2, rows // 4, width)
        mine = lax.dynamic_index_in_dim(shard, c, 0, keepdims=False)
        m0 = lax.dynamic_index_in_dim(mine, y, 0, keepdims=False)
        n0 = lax.dynamic_index_in_dim(mine, 1 - y, 0, keepdims=False)
        m1 = self.move(m0, self.up)
        m3 = self.move(m0, self.down)
        m2 = self.move(m1, self.up)
        first = [m0, m1, m2, m3]
        if light:
            second = [n0] + [self.move(piece, self.across_y) for piece in first[1:]]
        else:
            n1 = self.move(n0, self.up)
            n3 = self.move(n0, self.down)
            n2 = self.move(n3, self.down)
            second = [n0, n1, n2, n3]
        first += [self.move(piece, self.across_x) for piece in first]
        second += [self.move(piece, self.across_y) for piece in first[self.zs :]]
        pieces = [piece for pair in zip(first, second) for piece in pair]
        own = jnp.concatenate(pieces, axis=0)
        return own, self.move(own, self.core)

    def scatter(self, other, own_sum, light):
        y, c, _, _ = self.here()
        total = own_sum(self.move(other, self.core))
        rows, width = total.shape
        total = total.reshape(2, self.zs, 2, rows // (4 * self.zs), width)
        near, far = total[0], total[1]
        far_sum = low_sum(far[:, 0], self.move(far[:, 1], self.across_y))
        m = low_sum(near[:, 0], self.move(far_sum, self.across_x))
        n = near[:, 1]
        if light:
            back = self.move(n[1:], self.across_y)
            m = jnp.concatenate([m[:1], low_sum(m[1:], back)])
            n_done = n[0]
        else:
            n3 = low_sum(n[3], self.move(n[2], self.up))
            n_done = low_sum(n[0], self.move(n[1], self.down), self.move(n3, self.up))
        m1 = low_sum(m[1], self.move(m[2], self.down))
        m_done = low_sum(m[0], self.move(m[3], self.up), self.move(m1, self.down))
        crossed = self.move(jnp.stack([n_done, m_done]), self.across_y)
        done = low_sum(jnp.stack([m_done, n_done]), crossed)
        done = jnp.where(y == 0, done, done[::-1])
        done = jnp.stack([done, self.move(done, self.core)])
        done = jnp.where(c == 0, done, done[::-1]).astype(F32)
        return done.reshape(rows // (2 * self.zs) * 2, width)


class PlainPlan:
    def first_half(self):
        return jnp.int32(0)

    def to_own(self, values, halves):
        return values.reshape((2, -1) + values.shape[1:])

    def to_whole(self, values, halves):
        return values.reshape((-1,) + values.shape[2:])

    def gather(self, shard, light):
        full = lax.all_gather(shard, "mp", axis=0, tiled=True)
        return jnp.split(full, 2, axis=0)

    def scatter(self, other, own_sum, light):
        full = jnp.concatenate([own_sum(jnp.zeros_like(other)), other], axis=0)
        part = lax.psum_scatter(full, "mp", scatter_dimension=0, tiled=True)
        return lax.psum(part, "dp").astype(F32)


def dot_nt(left, right):
    return lax.dot_general(left, right, (((1,), (1,)), ((), ())), preferred_element_type=F32)


def dot_tn(left, right):
    return lax.dot_general(left, right, (((0,), (0,)), ((), ())), preferred_element_type=F32)


def dot_nn(left, right):
    return lax.dot_general(left, right, (((1,), (0,)), ((), ())), preferred_element_type=F32)


def forward_kernel(half, x_ref, w_ref, b_ref, window_ref, qk_ref, va_ref, soft_ref, sum_ref):
    first = half[0]
    samples, patches = soft_ref.shape[1], soft_ref.shape[2]
    grid_side = window_ref.shape[1]
    x = x_ref[...]
    w_qk = w_ref[0, first]
    w_vo = w_ref[0, 1 - first]
    qk = low(dot_nt(x, w_qk) + b_ref[0, 0:1])
    vo = low(dot_nt(x, w_vo) + b_ref[0, 1:2])
    qk_ref[0] = qk
    queries, keys, values = qk[:, :HS], qk[:, HS:], vo[:, :HS]
    window = window_ref[0]
    width = window.shape[1]
    bias = jnp.concatenate(
        [
            pltpu.roll(window, (width - (grid_side - 1 - row) * grid_side) % width, 1)[:, :patches]
            for row in range(grid_side)
        ],
        axis=0,
    )
    joined = []
    for sample in range(samples):
        rows = slice(sample * patches, (sample + 1) * patches)
        scores = dot_nt(queries[rows], keys[rows]) * HS ** (-0.5) + bias
        powers = jnp.exp(scores - jnp.max(scores, axis=-1, keepdims=True))
        soft = low(powers * (1.0 / jnp.sum(powers, axis=-1, keepdims=True)))
        soft_ref[0, sample] = soft
        attended = low(dot_nn(soft, values[rows]))
        joined.append(jnp.concatenate([values[rows], attended], axis=1))
    joined = jnp.concatenate(joined, axis=0)
    va_ref[0] = joined
    lane = lax.broadcasted_iota(jnp.int32, joined.shape, 1)
    part = dot_nn(jnp.where(lane < HS, jnp.zeros_like(joined), joined), w_vo)

    @pl.when(pl.program_id(0) == 0)
    def _():
        sum_ref[...] = part

    @pl.when(pl.program_id(0) > 0)
    def _():
        sum_ref[...] += part


def backward_kernel(
    half, x_ref, g_ref, w_ref, qk_ref, va_ref, soft_ref, dw_ref, db_ref, dwindow_ref, sum_ref
):
    first = half[0]
    samples, patches = soft_ref.shape[1], soft_ref.shape[2]
    grid_side = dwindow_ref.shape[1]
    x = x_ref[...]
    grad = g_ref[...]
    w_qk = w_ref[0, first]
    w_vo = w_ref[0, 1 - first]
    grad_attended = low(dot_nt(grad, w_vo))[:, HS:]
    qk = qk_ref[0]
    va = va_ref[0]
    queries, keys, values = qk[:, :HS], qk[:, HS:], va[:, :HS]
    score_sum = None
    grads_qk, grads_v = [], []
    for sample in range(samples):
        rows = slice(sample * patches, (sample + 1) * patches)
        soft = soft_ref[0, sample]
        grad_here = grad_attended[rows]
        grad_soft = dot_nt(grad_here, values[rows])
        grads_v.append(dot_tn(soft, grad_here))
        weighted = soft.astype(F32) * grad_soft
        grad_scores = weighted - soft.astype(F32) * jnp.sum(weighted, axis=-1, keepdims=True)
        grad_scores = low(grad_scores)
        wide = grad_scores.astype(F32)
        score_sum = wide if score_sum is None else score_sum + wide
        grad_q = dot_nn(grad_scores, keys[rows]) * HS ** (-0.5)
        grad_k = dot_tn(grad_scores, queries[rows]) * HS ** (-0.5)
        grads_qk.append(jnp.concatenate([grad_q, grad_k], axis=1))
    grad_qk = low(jnp.concatenate(grads_qk, axis=0))
    grad_v = low(jnp.concatenate(grads_v, axis=0))
    grad_vo = jnp.concatenate([grad_v, jnp.zeros_like(grad_v)], axis=1)
    dw_qk = low(dot_tn(grad_qk, x))
    dw_vo = low(jnp.concatenate([dot_tn(grad_v, x), dot_tn(va[:, HS:], grad)], axis=0))
    dw_ref[0, 0] = lax.select(first == 0, dw_qk, dw_vo)
    dw_ref[0, 1] = lax.select(first == 0, dw_vo, dw_qk)
    db_ref[0, 0:1] = jnp.sum(grad_qk.astype(F32), axis=0, keepdims=True)
    db_ref[0, 1:2] = jnp.sum(grad_vo.astype(F32), axis=0, keepdims=True)
    width = dwindow_ref.shape[2]
    window = jnp.zeros((grid_side, width), F32)
    blank = jnp.zeros((grid_side, width - patches), F32)
    for row in range(grid_side):
        band = score_sum[row * grid_side : (row + 1) * grid_side]
        window = window + pltpu.roll(
            jnp.concatenate([band, blank], axis=1), (grid_side - 1 - row) * grid_side, 1
        )
    dwindow_ref[0] = window
    part = dot_nn(grad_qk, w_qk) + dot_nn(grad_vo, w_vo)

    @pl.when(pl.program_id(0) == 0)
    def _():
        sum_ref[...] = part

    @pl.when(pl.program_id(0) > 0)
    def _():
        sum_ref[...] += part


def same(shape):
    return pl.BlockSpec(shape, lambda head, half: (0,) * len(shape))


def per_head(shape):
    return pl.BlockSpec((1,) + shape, lambda head, half: (head,) + (0,) * len(shape))


def attention_forward(half, rows_in, weights, bias, windows, patches):
    heads = weights.shape[0]
    count, width = rows_in.shape
    samples = count // patches
    flops = heads * 2 * count * (width * 6 * HS + patches * 2 * HS)
    return pl.pallas_call(
        forward_kernel,
        grid_spec=pltpu.PrefetchScalarGridSpec(
            num_scalar_prefetch=1,
            grid=(heads,),
            in_specs=[
                same(rows_in.shape),
                per_head(weights.shape[1:]),
                per_head(bias.shape[1:]),
                per_head(windows.shape[1:]),
            ],
            out_specs=[
                per_head((count, 2 * HS)),
                per_head((count, 2 * HS)),
                per_head((samples, patches, patches)),
                same(rows_in.shape),
            ],
        ),
        out_shape=[
            jax.ShapeDtypeStruct((heads, count, 2 * HS), BF16),
            jax.ShapeDtypeStruct((heads, count, 2 * HS), BF16),
            jax.ShapeDtypeStruct((heads, samples, patches, patches), BF16),
            jax.ShapeDtypeStruct((count, width), F32),
        ],
        compiler_params=pltpu.CompilerParams(vmem_limit_bytes=VMEM_BYTES),
        cost_estimate=pl.CostEstimate(
            flops=2 * flops, bytes_accessed=20 * 2**20, transcendentals=heads * count * patches
        ),
    )(half, rows_in, weights, bias, windows)


def attention_backward(half, rows_in, grad, weights, saved, window_shape, patches):
    heads = weights.shape[0]
    count, width = rows_in.shape
    samples = count // patches
    qk, va, soft = saved
    flops = heads * 2 * count * (width * 14 * HS + patches * 5 * HS)
    return pl.pallas_call(
        backward_kernel,
        grid_spec=pltpu.PrefetchScalarGridSpec(
            num_scalar_prefetch=1,
            grid=(heads,),
            in_specs=[
                same(rows_in.shape),
                same(grad.shape),
                per_head(weights.shape[1:]),
                per_head((count, 2 * HS)),
                per_head((count, 2 * HS)),
                per_head((samples, patches, patches)),
            ],
            out_specs=[
                per_head(weights.shape[1:]),
                per_head((2, 2 * HS)),
                per_head(window_shape),
                same(rows_in.shape),
            ],
        ),
        out_shape=[
            jax.ShapeDtypeStruct(weights.shape, BF16),
            jax.ShapeDtypeStruct((heads, 2, 2 * HS), F32),
            jax.ShapeDtypeStruct((heads,) + window_shape, F32),
            jax.ShapeDtypeStruct((count, width), F32),
        ],
        compiler_params=pltpu.CompilerParams(vmem_limit_bytes=VMEM_BYTES),
        cost_estimate=pl.CostEstimate(
            flops=2 * flops, bytes_accessed=30 * 2**20, transcendentals=0
        ),
    )(half, rows_in, grad, weights, qk, va, soft)


def displacement_entries(offset_index):
    side = int(round(offset_index.shape[0] ** 0.5))
    by_place = offset_index.reshape(side, side, side, side)
    rows = jnp.concatenate(
        [by_place[0, :, :0:-1, :].transpose(1, 0, 2), by_place[:, :, 0, :]], axis=0
    )
    return jnp.concatenate([rows[:, 0, :0:-1], rows[:, :, 0]], axis=1)


def column_selector(side):
    places = jnp.arange(side)
    shift = places[:, None] - places[None, :] + side - 1
    return jnp.arange(2 * side - 1)[:, None] == shift.reshape(1, side * side)


def table_windows(table, entries):
    span = entries.shape[0]
    side = (span + 1) // 2
    heads = table.shape[1]
    pick = entries.reshape(-1, 1) == jnp.arange(table.shape[0])[None, :]
    ordered = jnp.dot(low(pick), table, preferred_element_type=F32)
    ordered = ordered.reshape(span, span, heads)[::-1].transpose(2, 0, 1)
    spread = jnp.dot(low(ordered).reshape(-1, span), low(column_selector(side)), preferred_element_type=F32)
    spread = spread.reshape(heads, span, side, side).transpose(0, 2, 1, 3)
    spread = spread.reshape(heads, side, span * side)
    return jnp.pad(spread, ((0, 0), (0, 0), (0, side)))


def table_from_windows(windows, entries, table_rows):
    span = entries.shape[0]
    heads, side, _ = windows.shape
    spread = windows[:, :, : span * side].reshape(heads, side, span, side).transpose(0, 2, 1, 3)
    spread = spread.reshape(heads * span, side * side)
    ordered = jnp.dot(spread, column_selector(side).astype(F32).T, precision=HIGHEST)
    ordered = ordered.reshape(heads, span, span)[:, ::-1].reshape(heads, span * span)
    pick = entries.reshape(-1, 1) == jnp.arange(table_rows)[None, :]
    return jnp.dot(ordered, pick.astype(F32), precision=HIGHEST)


def normalize(values):
    centred = values - jnp.mean(values, axis=-1, keepdims=True)
    inverse = lax.rsqrt(jnp.mean(centred * centred, axis=-1, keepdims=True) + EPSILON)
    return (centred * inverse, inverse)


def norm_back(grad_normed, normed, inverse):
    first_mean = jnp.mean(grad_normed, axis=-1, keepdims=True)
    second_mean = jnp.mean(grad_normed * normed, axis=-1, keepdims=True)
    return (grad_normed - first_mean - normed * second_mean) * inverse


def attention_rows(qkv_weight, out_weight):
    width, _, local_width = qkv_weight.shape
    heads = local_width // HS
    qkv = qkv_weight.reshape(width, 3, heads, HS).transpose(2, 1, 3, 0)
    out = out_weight.reshape(heads, 1, HS, width)
    return jnp.concatenate([qkv, out], axis=1).reshape(heads * 4 * HS, width)


def local(
    plan,
    tokens,
    conditioning,
    counts,
    offset_index,
    modulator,
    modulator_bias,
    qkv_weight,
    qv_bias,
    offset_table,
    out_weight,
    out_bias,
    up_weight,
    up_bias,
    down_weight,
    down_bias,
    out_grad,
):
    rows, width = tokens.shape
    patches = offset_index.shape[0]
    samples = rows // patches
    group_samples = conditioning.shape[0]
    shards = group_samples // samples
    columns = modulator.shape[1]
    local_width = qkv_weight.shape[2]
    local_heads = local_width // HS
    table_rows = offset_table.shape[0]
    local_units = up_weight.shape[1]
    heads = local_heads * shards

    half = plan.first_half().reshape(1)
    attn_w = plan.gather(attention_rows(qkv_weight, out_weight), True)
    up_w = plan.gather(up_weight.T, False)
    down_w = plan.gather(down_weight, False)

    small = jnp.concatenate([qv_bias.reshape(-1), offset_table.reshape(-1), up_bias])
    small = lax.all_gather(small, "mp", axis=0)
    cut_one, cut_two = 2 * local_width, 2 * local_width + table_rows * local_heads
    all_qv = small[:, :cut_one].reshape(shards, 2, local_heads, HS).transpose(0, 2, 1, 3)
    all_qv = all_qv.reshape(heads, 2, HS).astype(F32)
    all_qv = jnp.concatenate([all_qv, jnp.zeros_like(all_qv)], axis=2)
    head_bias = plan.to_own(all_qv, False)
    table = small[:, cut_one:cut_two].reshape(shards, table_rows, local_heads)
    table = table.transpose(1, 0, 2).reshape(table_rows, heads)
    entries = displacement_entries(offset_index)
    windows = plan.to_own(table_windows(table, entries), False)
    up_biases = plan.to_own(small[:, cut_two:].reshape(-1).astype(F32), True)

    cond_float = conditioning.astype(F32)
    activated = low(jax.nn.silu(cond_float))
    mod_part = jnp.dot(activated, modulator, preferred_element_type=F32) + modulator_bias.astype(F32)
    mod_own = lax.all_to_all(mod_part.reshape(shards, samples, columns), "mp", 0, 0)
    mod_own = mod_own.transpose(1, 0, 2).reshape(samples, 6, 1, width)
    shift_one, scale_one, gate_one, shift_two, scale_two, gate_two = [mod_own[:, n] for n in range(6)]
    all_activated = lax.all_gather(activated, "dp", axis=0, tiled=True)

    sample_number = lax.axis_index("mp") * samples + jnp.arange(samples, dtype=jnp.int32)
    live = (sample_number < counts[0]).astype(F32)[:, None, None]

    by_sample = (samples, patches, width)
    flat = (rows, width)
    tokens_float = tokens.reshape(by_sample).astype(F32)
    normed_one, inverse_one = normalize(tokens_float)
    input_one = low(normed_one * (1.0 + scale_one) + shift_one).reshape(flat)

    head_shape = (heads // 2, 2, 2 * HS, width)
    attn_w = [part.reshape(head_shape) for part in attn_w]
    saved = []
    attn_branch = out_bias.astype(F32)
    for part in range(2):
        *kept, branch = attention_forward(
            half, input_one, attn_w[part], head_bias[part], windows[part], patches
        )
        saved.append(kept)
        attn_branch = attn_branch + branch.reshape(by_sample)
    mid_tokens = tokens_float + gate_one * attn_branch
    normed_two, inverse_two = normalize(mid_tokens)
    input_two = low(normed_two * (1.0 + scale_two) + shift_two).reshape(flat)

    grad_final = out_grad.reshape(by_sample).astype(F32) * live
    mlp_grad = low(gate_two * grad_final).reshape(flat)

    pre_act = [dot_nt(input_two, up_w[part]) + up_biases[part] for part in range(2)]
    hidden = [low(jax.nn.gelu(value, approximate=True)) for value in pre_act]
    down_shard = plan.scatter(
        low(dot_tn(hidden[1], mlp_grad)),
        lambda came: low(dot_tn(hidden[0], mlp_grad) + came.astype(F32)),
        False,
    )
    mlp_branch = dot_nn(hidden[0], down_w[0]) + dot_nn(hidden[1], down_w[1])
    mlp_branch = (mlp_branch + down_bias.astype(F32)).reshape(by_sample)
    block_out = low((mid_tokens + gate_two * mlp_branch) * live).reshape(flat)

    grad_pre = []
    for part in range(2):
        _, gelu_back = jax.vjp(partial(jax.nn.gelu, approximate=True), pre_act[part])
        grad_pre.append(low(gelu_back(dot_nt(mlp_grad, down_w[part]))[0]))
    grad_input_two = dot_nn(grad_pre[0], up_w[0]) + dot_nn(grad_pre[1], up_w[1])
    grad_input_two = grad_input_two.reshape(by_sample)
    up_shard = plan.scatter(
        low(dot_tn(grad_pre[1], input_two)),
        lambda came: low(dot_tn(grad_pre[0], input_two) + came.astype(F32)),
        False,
    )
    grad_mid = grad_final + norm_back(grad_input_two * (1.0 + scale_two), normed_two, inverse_two)
    attn_grad = low(gate_one * grad_mid).reshape(flat)

    window_shape = windows.shape[2:]
    back = [None, None]
    for part in (1, 0):
        back[part] = attention_backward(
            half, input_one, attn_grad, attn_w[part], saved[part], window_shape, patches
        )
    attn_rows = (heads // 2 * 4 * HS, width)
    attn_shard = plan.scatter(
        back[1][0].reshape(attn_rows),
        lambda came: low_sum(back[0][0].reshape(attn_rows), came),
        True,
    )
    grad_input_one = (back[0][3] + back[1][3]).reshape(by_sample)
    tokens_grad = grad_mid + norm_back(grad_input_one * (1.0 + scale_one), normed_one, inverse_one)

    mod_grad = jnp.stack(
        [
            jnp.sum(value, axis=1)
            for value in (
                grad_input_one,
                grad_input_one * normed_one,
                grad_mid * attn_branch,
                grad_input_two,
                grad_input_two * normed_two,
                grad_final * mlp_branch,
            )
        ],
        axis=1,
    )
    mod_grad = low(mod_grad).reshape(samples, shards, columns).transpose(1, 0, 2)
    mod_grad = lax.all_to_all(mod_grad, "mp", 0, 0).reshape(group_samples, columns)
    act_grad = lax.psum(low(dot_nt(mod_grad, modulator)), "mp").astype(F32)
    _, silu_back = jax.vjp(jax.nn.silu, cond_float)
    cond_grad = silu_back(act_grad)[0]
    all_mod_grad = lax.all_gather(mod_grad, "dp", axis=0, tiled=True)
    modulator_grad = dot_tn(all_activated, all_mod_grad)
    modulator_bias_grad = jnp.sum(all_mod_grad.astype(F32), axis=0)

    head_grads = plan.to_whole(jnp.stack([back[0][1], back[1][1]]), False)[:, :, :HS]
    window_grads = plan.to_whole(jnp.stack([back[0][2], back[1][2]]), False)
    table_grads = table_from_windows(window_grads, entries, table_rows)
    up_bias_grads = jnp.stack([jnp.sum(part.astype(F32), axis=0) for part in grad_pre])
    up_bias_grads = plan.to_whole(up_bias_grads, True)
    totals = lax.psum(
        jnp.concatenate(
            [
                head_grads.reshape(-1),
                table_grads.reshape(-1),
                up_bias_grads,
                jnp.sum(attn_grad.astype(F32), axis=0),
                jnp.sum(mlp_grad.astype(F32), axis=0),
            ]
        ),
        BOTH,
    )
    place = lax.axis_index("mp")

    def my_part(start, size):
        return lax.dynamic_slice_in_dim(totals, start + place * size, size)

    head_size = 2 * heads * HS
    table_size = heads * table_rows
    units = shards * local_units
    qv_bias_grad = my_part(0, head_size // shards).reshape(local_heads, 2, HS)
    qv_bias_grad = qv_bias_grad.transpose(1, 0, 2).reshape(2, local_width)
    offset_table_grad = my_part(head_size, table_size // shards).reshape(local_heads, table_rows).T
    up_bias_grad = my_part(head_size + table_size, local_units)
    tail = head_size + table_size + units
    out_bias_grad = totals[tail : tail + width]
    down_bias_grad = totals[tail + width :]

    attn_shard = attn_shard.reshape(local_heads, 4, HS, width)
    qkv_grad = attn_shard[:, :3].transpose(3, 1, 0, 2).reshape(width, 3, local_width)
    out_weight_grad = attn_shard[:, 3].reshape(local_width, width)
    return (
        block_out,
        tokens_grad.reshape(flat),
        cond_grad,
        modulator_grad,
        modulator_bias_grad,
        qkv_grad,
        qv_bias_grad,
        offset_table_grad,
        out_weight_grad,
        out_bias_grad,
        up_shard.T,
        up_bias_grad,
        down_shard,
        down_bias_grad,
    )


def solution(mesh):
    known = (mesh.shape["dp"], mesh.shape["mp"]) == (4, 8)
    plan = PairPlan(mesh) if known else PlainPlan()
    in_specs = (
        P(("dp", "mp"), None),
        P("dp", None),
        P("dp"),
        P(),
        P(None, "mp"),
        P("mp"),
        P(None, None, "mp"),
        P(None, "mp"),
        P(None, "mp"),
        P("mp", None),
        P(),
        P(None, "mp"),
        P("mp"),
        P("mp", None),
        P(),
        P(("dp", "mp"), None),
    )
    out_specs = (
        P(("dp", "mp"), None),
        P(("dp", "mp"), None),
        P("dp", None),
        P(None, "mp"),
        P("mp"),
        P(None, None, "mp"),
        P(None, "mp"),
        P(None, "mp"),
        P("mp", None),
        P(),
        P(None, "mp"),
        P("mp"),
        P("mp", None),
        P(),
    )
    return jax.shard_map(
        partial(local, plan), mesh=mesh, in_specs=in_specs, out_specs=out_specs, check_vma=False
    )
```

```python
from functools import partial

import jax
import jax.numpy as jnp
from jax import lax
from jax.experimental import pallas as pl
from jax.experimental.pallas import tpu as pltpu
from jax.sharding import PartitionSpec as P

HS = 72
EPSILON = 1e-06
HIGHEST = lax.Precision.HIGHEST
BOTH = ("dp", "mp")
VMEM_BYTES = 44 * 2**20
BF16 = jnp.bfloat16
F32 = jnp.float32


def low(value):
    return value.astype(BF16)


def low_sum(*values):
    total = values[0].astype(F32)
    for value in values[1:]:
        total = total + value.astype(F32)
    return low(total)


def together(moved, held):
    return lax.optimization_barrier((moved, held))


class Step:
    def __init__(self, holder):
        self.holder = holder

    def __call__(self, moves, *names):
        moved = [lax.ppermute(value, BOTH, way) for value, way in moves]
        held = [getattr(self.holder, name) for name in names]
        moved, held = together(moved, held)
        for name, value in zip(names, held):
            setattr(self.holder, name, value)
        return moved


class GroupSum:
    def __init__(self):
        self.near_m, self.near_n, self.far_m, self.far_n = {}, {}, {}, {}

    def near(self, k, own, came):
        self.near_m[k], self.near_n[k] = [own[0], came[0]], [own[1], came[1]]

    def far(self, k, own, came):
        self.far_m[k], self.far_n[k] = [own[0], came[0]], [own[1], came[1]]

    def send(self, *terms):
        return jnp.stack([low_sum(*term) for term in terms])

    def done_pair(self):
        self.kept = self.send(self.near_n[0], self.near_m[0])
        return self.kept

    def done(self, crossed):
        return low_sum(self.kept[::-1], crossed)


class PairPlan:
    chunks = (((0, 0), (0, 1)), ((1, 0), (3, 0)), ((1, 1), (3, 1)), ((2, 0), (2, 1)))

    def __init__(self, mesh):
        self.zs = mesh.shape["mp"] // 2
        zs = self.zs
        self.core = self.moves(lambda y, c, z, x: (y, 1 - c, z, x))
        self.across_x = self.moves(lambda y, c, z, x: (y, c, z, 1 - x))
        self.across_y = self.moves(lambda y, c, z, x: (1 - y, c, z, x))
        self.up = self.moves(lambda y, c, z, x: (y, c, (z + 1) % zs, x))
        self.down = self.moves(lambda y, c, z, x: (y, c, (z - 1) % zs, x))

    def moves(self, target):
        def number(y, c, z, x):
            return ((y * 2 + c) * self.zs + z) * 2 + x

        places = [(y, c, z, x) for y in (0, 1) for c in (0, 1) for z in range(self.zs) for x in (0, 1)]
        return [(number(*place), number(*target(*place))) for place in places]

    def here(self):
        dp, mp = lax.axis_index("dp"), lax.axis_index("mp")
        return dp // 2, dp % 2, mp // 2, mp % 2

    def first_half(self):
        return self.here()[0]

    def turned(self, values, halves):
        y, c, z, x = self.here()
        places = jnp.arange(self.zs)
        pick = (places[:, None] + places[None, :]) % self.zs == z
        pick = pick.reshape(pick.shape + (1,) * (values.ndim - 1))
        values = jnp.sum(jnp.where(pick, values[None], jnp.zeros_like(values[None])), axis=1)
        values = jnp.where(x == 0, values, values[:, ::-1])
        values = jnp.where(c == 0, values, values[:, :, ::-1])
        if halves:
            values = jnp.where(y == 0, values, values[:, :, :, ::-1])
        return values

    def to_own(self, values):
        rest = values.shape[1:]
        split = self.turned(values.reshape((self.zs, 2, 2) + rest), False)
        split = split.transpose((2, 0, 1) + tuple(range(3, split.ndim)))
        return split.reshape((2, values.shape[0] // 2) + rest)

    def to_whole(self, values):
        rest = values.shape[2:]
        split = values.reshape((2, self.zs, 2) + rest)
        split = split.transpose((1, 2, 0) + tuple(range(3, split.ndim)))
        return self.turned(split, False).reshape((-1,) + rest)

    def units_to_whole(self, values):
        split = self.turned(values.reshape(self.zs, 2, 2, 2, -1), True)
        return split.transpose(0, 1, 3, 2, 4).reshape(-1)

    def unit_order(self):
        y, c, z, x = self.here()
        shards = [((z - k) % self.zs) * 2 + (x ^ j) for k in range(self.zs) for j in range(2)]
        quarters = [(y ^ half) * 2 + (c ^ core) for core in range(2) for half in range(2)]
        return jnp.stack(shards).astype(jnp.int32), jnp.stack(quarters).astype(jnp.int32)

    def chunk(self, number, values):
        return jnp.stack([values[2 * k + j] for k, j in self.chunks[number]])

    def in_slots(self, parts):
        slots = {}
        for number, part in enumerate(parts):
            for place, (k, j) in enumerate(self.chunks[number]):
                slots[2 * k + j] = part[place]
        return jnp.stack([slots[place] for place in range(len(slots))])

    def pieces(self, shard, core_first):
        y, c, _, _ = self.here()
        rows, width = shard.shape
        split = shard.reshape(2, 2, rows // 4, width)
        mine = lax.dynamic_index_in_dim(split, c, 0 if core_first else 1, keepdims=False)
        return jnp.where(y == 0, mine, mine[::-1])

    def whole_shard(self, mine, others, core_first):
        y, c, _, _ = self.here()
        both = jnp.stack([mine, others])
        both = jnp.where(y == 0, both, both[:, ::-1])
        both = jnp.where(c == 0, both, both[::-1])
        both = both if core_first else both.transpose(1, 0, 2, 3)
        return both.reshape(-1, both.shape[-1]).astype(F32)

    def sum_groups(self, value):
        value = value + lax.ppermute(value, BOTH, self.core)
        return value + lax.ppermute(value, BOTH, self.across_y)

    def gather_groups(self, value):
        y, c, _, _ = self.here()
        other = lax.ppermute(value, BOTH, self.core)
        both = jnp.where(c == 0, jnp.stack([value, other]), jnp.stack([other, value]))
        other = lax.ppermute(both, BOTH, self.across_y)
        both = jnp.where(y == 0, jnp.stack([both, other]), jnp.stack([other, both]))
        return both.reshape((-1,) + value.shape[1:])

    def run(self, work):
        step = Step(work)
        up, down, x, y, core = self.up, self.down, self.across_x, self.across_y, self.core
        stack = lambda *values: jnp.stack(values)
        attn = self.pieces(work.attn_rows, True)
        feed = self.pieces(work.down_rows, False)
        quarters = work.up_rows.reshape(4, -1, work.width)
        work.quarter = lax.dynamic_index_in_dim(quarters, lax.axis_index("dp"), 0, keepdims=False)

        work.modulate()
        a1, a3, f0 = step(
            [(attn[0], up), (attn[0], down), (attn, x)], "modulation", "tokens", "small", "offset_index", "quarter"
        )
        work.norm_one()
        work.gather_small()
        own = stack(attn, f0)
        a2, n1, xm3, other, d1 = step(
            [(a1, up), (a1, y), (a3, x), (own, core), (feed, up)], "input_one", "gathered_small", "quarter"
        )
        work.up_w = lax.all_gather(work.quarter, ("mp", "dp"), axis=0, tiled=True)
        work.forward_weights(0, own, other)
        work.prepare()
        near1 = stack(a1, n1)
        far1, came3, d3 = step([(near1, x), (stack(a3, xm3), y), (feed, down)], "windows", "input_one")
        near3, far3 = stack(a3, came3[0]), stack(xm3, came3[1])
        work.forward(0)
        own1, own2 = stack(near1, near3), stack(far1, far3)
        (xm2, dx0), dm2, dn2, other1, other2 = step(
            [(stack(a2, feed[0]), x), (d1[0], up), (d3[1], down), (own1, core), (own2, core)],
            "branch",
            "input_one",
        )
        work.forward_weights(1, own1, other1)
        work.forward_weights(2, own2, other2)
        work.forward(1)
        (n2, xn2, dy0), (dx1, dx3) = step(
            [(stack(a2, xm2, dx0), y), (stack(d1[0], d3[0]), x)], "branch", "input_one"
        )
        own3 = stack(stack(a2, n2), stack(xm2, xn2))
        work.forward(2)
        other3, dx2, (dy1, dy3) = step(
            [(own3, core), (dm2, x), (stack(dx1, dx3), y)], "branch", "input_one"
        )
        work.forward_weights(3, own3, other3)
        work.forward(3)
        down_own = [stack(feed, stack(dx0, dy0), d1, stack(dx1, dy1))]
        dy2, other_down = step([(dx2, y), (down_own[0], core)], "branch", "up_w")
        down_other = [other_down]
        work.norm_two()
        down_own.append(stack(stack(dm2, dn2), stack(dx2, dy2), d3, stack(dx3, dy3)))
        (other_down,) = step([(down_own[1], core)], "input_two", "mlp_grad")
        down_other.append(other_down)
        work.down_w = list(zip(down_own, down_other))
        work.units_forward()
        step([], "hidden", "slope", "down_grad", "units_in")

        work.down_part = lax.psum_scatter(
            work.down_grad.reshape(-1, work.width), ("mp", "dp"), scatter_dimension=0, tiled=True
        )
        units, heads = GroupSum(), GroupSum()

        def add_units(part, came):
            for k in (0, 1):
                own = work.up_grads[part][0]
                units.near(2 * part + k, own[2 * k], came[2 * k])
                units.far(2 * part + k, own[2 * k + 1], came[2 * k + 1])

        def add_heads(number, came):
            own = work.head_grads[number][0]
            for place, (k, j) in enumerate(self.chunks[number]):
                (heads.far if j else heads.near)(k, own[place], came[place])

        work.units_backward(0)
        step([], "up_grads", "units_in")
        work.units_backward(1)
        (came,) = step([(work.up_grads[0][1], core)], "up_grads", "grad_input_two_parts")
        add_units(0, came)
        work.norm_two_back()
        far0, got1, n1, came = step(
            [
                (units.send(units.far_m[0], units.far_n[0]), x),
                (units.send(units.far_n[1]), y),
                (units.send(units.near_n[1]), down),
                (work.up_grads[1][1], core),
            ],
            "attn_grad",
        )
        add_units(1, came)
        units.near_m[0].append(far0[0])
        units.near_n[0] += [far0[1], n1[0]]
        units.far_m[1].append(got1[0])
        work.backward(3)
        far1, got23, n2 = step(
            [
                (units.send(units.far_m[1]), x),
                (units.send(units.far_n[2], units.far_n[3]), y),
                (units.send(units.near_n[2]), up),
            ],
            "attn_grad",
            "head_grads",
        )
        units.near_m[1].append(far1[0])
        for place, k in enumerate((2, 3)):
            units.far_m[k].append(got23[place])
        units.near_n[3].append(n2[0])
        work.backward(2)
        far23, n3, came = step(
            [
                (units.send(units.far_m[2], units.far_m[3]), x),
                (units.send(units.near_n[3]), up),
                (work.head_grads[3][1], core),
            ],
            "attn_grad",
            "head_grads",
        )
        for place, k in enumerate((2, 3)):
            units.near_m[k].append(far23[place])
        units.near_n[0].append(n3[0])
        add_heads(3, came)
        work.backward(1)
        m2, m3, got2, came = step(
            [
                (units.send(units.near_m[2]), down),
                (units.send(units.near_m[3]), up),
                (heads.send(heads.far_n[2], heads.near_n[2]), y),
                (work.head_grads[2][1], core),
            ],
            "attn_grad",
            "head_grads",
        )
        units.near_m[1].append(m2[0])
        units.near_m[0].append(m3[0])
        heads.far_m[2].append(got2[0])
        heads.near_m[2].append(got2[1])
        add_heads(2, came)
        work.backward(0)
        m1, far2, got13, came = step(
            [
                (units.send(units.near_m[1]), down),
                (heads.send(heads.far_m[2]), x),
                (heads.send(heads.far_n[1], heads.far_n[3]), y),
                (work.head_grads[1][1], core),
            ],
            "hidden",
            "head_grads",
            "rows_grads",
            "down_part",
        )
        units.near_m[0].append(m1[0])
        heads.near_m[2].append(far2[0])
        for place, k in enumerate((1, 3)):
            heads.far_m[k].append(got13[place])
        add_heads(1, came)
        work.units_out()
        far13, got13, m2, came = step(
            [
                (heads.send(heads.far_m[1], heads.far_m[3]), x),
                (heads.send(heads.near_n[1], heads.near_n[3]), y),
                (heads.send(heads.near_m[2]), down),
                (work.head_grads[0][1], core),
            ],
            "mlp_parts",
            "rows_grads",
        )
        for place, k in enumerate((1, 3)):
            heads.near_m[k] += [far13[place], got13[place]]
        heads.near_m[1].append(m2[0])
        add_heads(0, came)
        work.finish_rows()
        far0, crossed, m3, m1 = step(
            [
                (heads.send(heads.far_m[0], heads.far_n[0]), x),
                (units.done_pair(), y),
                (heads.send(heads.near_m[3]), up),
                (heads.send(heads.near_m[1]), down),
            ],
            "sums",
            "mod_grad",
            "tokens_grad",
            "block_out",
        )
        heads.near_m[0] += [far0[0], m3[0], m1[0]]
        heads.near_n[0].append(far0[1])
        up_mine = units.done(crossed)
        work.finish_small()
        crossed, up_other = step([(heads.done_pair(), y), (up_mine, core)])
        attn_mine = heads.done(crossed)
        (attn_other,) = step([(attn_mine, core)])
        work.up_shard = self.whole_shard(up_mine, up_other, False)
        work.attn_shard = self.whole_shard(attn_mine, attn_other, True)
        work.down_shard = lax.all_gather(work.down_part, "dp", axis=0, tiled=True).astype(F32)


class PlainPlan:
    def __init__(self, mesh):
        self.shards = mesh.shape["mp"]

    def first_half(self):
        return jnp.int32(0)

    def to_own(self, values):
        return values.reshape((2, -1) + values.shape[1:])

    def to_whole(self, values):
        return values.reshape((-1,) + values.shape[2:])

    def units_to_whole(self, values):
        return values.reshape(-1)

    def unit_order(self):
        return jnp.arange(self.shards, dtype=jnp.int32), jnp.arange(4, dtype=jnp.int32)

    def chunk(self, number, values):
        return values

    def in_slots(self, parts):
        return parts[0]

    def sum_groups(self, value):
        return lax.psum(value, "dp")

    def gather_groups(self, value):
        return lax.all_gather(value, "dp", axis=0, tiled=True)

    def gather(self, shard):
        return lax.all_gather(shard, "mp", axis=0, tiled=True)

    def scatter(self, full):
        full = full.reshape(-1, full.shape[-1])
        part = lax.psum_scatter(full, "mp", scatter_dimension=0, tiled=True)
        return lax.psum(part, "dp").astype(F32)

    def run(self, work):
        work.modulate()
        work.norm_one()
        work.gather_small()
        work.prepare()
        attn = self.gather(work.attn_rows).reshape(2, -1, 2, 2 * HS, work.width)
        work.forward_weights(0, attn[0], attn[1])
        work.forward(0)
        work.norm_two()
        work.up_w = self.gather(work.up_rows)
        feed = self.gather(work.down_rows)
        feed = feed.reshape(2, self.shards // 2, 2, 2, -1, work.width)
        work.down_w = [(part[:, 0], part[:, 1]) for part in feed]
        work.units_forward()
        work.down_shard = self.scatter(work.down_grad)
        for part in (0, 1):
            work.units_backward(part)
        work.norm_two_back()
        up_grads = [jnp.stack(pair, axis=1) for pair in work.up_grads]
        work.up_shard = self.scatter(jnp.concatenate(up_grads))
        work.backward(0)
        work.attn_shard = self.scatter(jnp.stack(work.head_grads[0]))
        work.units_out()
        work.finish_rows()
        work.finish_small()


def dot_nt(left, right):
    return lax.dot_general(left, right, (((1,), (1,)), ((), ())), preferred_element_type=F32)


def dot_tn(left, right):
    return lax.dot_general(left, right, (((0,), (0,)), ((), ())), preferred_element_type=F32)


def dot_nn(left, right):
    return lax.dot_general(left, right, (((1,), (0,)), ((), ())), preferred_element_type=F32)


def forward_head(half, x_ref, w_ref, b_ref, window_ref, qk_ref, va_ref, soft_ref):
    first = half[0]
    samples, patches = soft_ref.shape[1], soft_ref.shape[2]
    grid_side = window_ref.shape[1]
    x = x_ref[...]
    w_qk = w_ref[0, first]
    w_vo = w_ref[0, 1 - first]
    qk = low(dot_nt(x, w_qk) + b_ref[0, 0:1])
    vo = low(dot_nt(x, w_vo) + b_ref[0, 1:2])
    qk_ref[0] = qk
    queries, keys, values = qk[:, :HS], qk[:, HS:], vo[:, :HS]
    window = window_ref[0]
    width = window.shape[1]
    bias = jnp.concatenate(
        [
            pltpu.roll(window, (width - (grid_side - 1 - row) * grid_side) % width, 1)[:, :patches]
            for row in range(grid_side)
        ],
        axis=0,
    )
    joined = []
    for sample in range(samples):
        rows = slice(sample * patches, (sample + 1) * patches)
        scores = dot_nt(queries[rows], keys[rows]) * HS ** (-0.5) + bias
        powers = jnp.exp(scores - jnp.max(scores, axis=-1, keepdims=True))
        soft = low(powers * (1.0 / jnp.sum(powers, axis=-1, keepdims=True)))
        soft_ref[0, sample] = soft
        attended = low(dot_nn(soft, values[rows]))
        joined.append(jnp.concatenate([values[rows], attended], axis=1))
    joined = jnp.concatenate(joined, axis=0)
    va_ref[0] = joined
    lane = lax.broadcasted_iota(jnp.int32, joined.shape, 1)
    return dot_nn(jnp.where(lane < HS, jnp.zeros_like(joined), joined), w_vo)


def add_up(sum_ref, part):
    @pl.when(pl.program_id(0) == 0)
    def _():
        sum_ref[...] = part

    @pl.when(pl.program_id(0) > 0)
    def _():
        sum_ref[...] += part


def forward_kernel(half, x_ref, *refs):
    ins, outs, sum_ref = refs[:6], refs[6:12], refs[12]
    part = forward_head(half, x_ref, *ins[:3], *outs[:3])
    part += forward_head(half, x_ref, *ins[3:], *outs[3:])
    add_up(sum_ref, part)


def backward_head(
    half, x_ref, g_ref, w_ref, qk_ref, va_ref, soft_ref, dw_ref, db_ref, dwindow_ref
):
    first = half[0]
    samples, patches = soft_ref.shape[1], soft_ref.shape[2]
    grid_side = dwindow_ref.shape[1]
    x = x_ref[...]
    grad = g_ref[...]
    w_qk = w_ref[0, first]
    w_vo = w_ref[0, 1 - first]
    grad_attended = low(dot_nt(grad, w_vo))[:, HS:]
    qk = qk_ref[0]
    va = va_ref[0]
    queries, keys, values = qk[:, :HS], qk[:, HS:], va[:, :HS]
    score_sum = None
    grads_qk, grads_v = [], []
    for sample in range(samples):
        rows = slice(sample * patches, (sample + 1) * patches)
        soft = soft_ref[0, sample]
        grad_here = grad_attended[rows]
        grad_soft = dot_nt(grad_here, values[rows])
        grads_v.append(dot_tn(soft, grad_here))
        weighted = soft.astype(F32) * grad_soft
        grad_scores = weighted - soft.astype(F32) * jnp.sum(weighted, axis=-1, keepdims=True)
        grad_scores = low(grad_scores)
        wide = grad_scores.astype(F32)
        score_sum = wide if score_sum is None else score_sum + wide
        grad_q = dot_nn(grad_scores, keys[rows]) * HS ** (-0.5)
        grad_k = dot_tn(grad_scores, queries[rows]) * HS ** (-0.5)
        grads_qk.append(jnp.concatenate([grad_q, grad_k], axis=1))
    grad_qk = low(jnp.concatenate(grads_qk, axis=0))
    grad_v = low(jnp.concatenate(grads_v, axis=0))
    grad_vo = jnp.concatenate([grad_v, jnp.zeros_like(grad_v)], axis=1)
    dw_qk = low(dot_tn(grad_qk, x))
    dw_vo = low(jnp.concatenate([dot_tn(grad_v, x), dot_tn(va[:, HS:], grad)], axis=0))
    dw_ref[0, 0] = lax.select(first == 0, dw_qk, dw_vo)
    dw_ref[0, 1] = lax.select(first == 0, dw_vo, dw_qk)
    db_ref[0, 0:1] = jnp.sum(grad_qk.astype(F32), axis=0, keepdims=True)
    db_ref[0, 1:2] = jnp.sum(grad_vo.astype(F32), axis=0, keepdims=True)
    width = dwindow_ref.shape[2]
    window = jnp.zeros((grid_side, width), F32)
    blank = jnp.zeros((grid_side, width - patches), F32)
    for row in range(grid_side):
        band = score_sum[row * grid_side : (row + 1) * grid_side]
        window = window + pltpu.roll(
            jnp.concatenate([band, blank], axis=1), (grid_side - 1 - row) * grid_side, 1
        )
    dwindow_ref[0] = window
    return dot_nn(grad_qk, w_qk) + dot_nn(grad_vo, w_vo)


def backward_kernel(half, x_ref, g_ref, *refs):
    ins, outs, sum_ref = refs[:8], refs[8:14], refs[14]
    part = backward_head(half, x_ref, g_ref, *ins[:4], *outs[:3])
    part += backward_head(half, x_ref, g_ref, *ins[4:], *outs[3:])
    add_up(sum_ref, part)


def same(shape):
    return pl.BlockSpec(shape, lambda head, half: (0,) * len(shape))


def per_head(shape):
    return pl.BlockSpec((1,) + shape, lambda head, half: (head,) + (0,) * len(shape))


def attention_forward(half, rows_in, weights, bias, windows, patches):
    heads = weights[0].shape[0]
    count, width = rows_in.shape
    samples = count // patches
    flops = heads * 4 * count * (width * 6 * HS + patches * 2 * HS)
    shapes = ((count, 2 * HS), (count, 2 * HS), (samples, patches, patches))
    *saved, branch = pl.pallas_call(
        forward_kernel,
        grid_spec=pltpu.PrefetchScalarGridSpec(
            num_scalar_prefetch=1,
            grid=(heads,),
            in_specs=[same(rows_in.shape)]
            + [per_head(value[0].shape[1:]) for value in (weights, bias, windows)] * 2,
            out_specs=[per_head(shape) for shape in shapes] * 2 + [same(rows_in.shape)],
        ),
        out_shape=[jax.ShapeDtypeStruct((heads,) + shape, BF16) for shape in shapes] * 2
        + [jax.ShapeDtypeStruct((count, width), F32)],
        compiler_params=pltpu.CompilerParams(vmem_limit_bytes=VMEM_BYTES),
        cost_estimate=pl.CostEstimate(
            flops=2 * flops, bytes_accessed=heads * 6 * 2**20, transcendentals=2 * heads * count * patches
        ),
    )(half, rows_in, *[value[part] for part in (0, 1) for value in (weights, bias, windows)])
    return (saved[:3], saved[3:]), branch


def attention_backward(half, rows_in, grad, weights, saved, window_shape, patches):
    heads = weights[0].shape[0]
    count, width = rows_in.shape
    samples = count // patches
    flops = heads * 4 * count * (width * 14 * HS + patches * 5 * HS)
    shapes = ((count, 2 * HS), (count, 2 * HS), (samples, patches, patches))
    results = ((weights[0].shape[1:], BF16), ((2, 2 * HS), F32), (window_shape, F32))
    *out, rows_grad = pl.pallas_call(
        backward_kernel,
        grid_spec=pltpu.PrefetchScalarGridSpec(
            num_scalar_prefetch=1,
            grid=(heads,),
            in_specs=[same(rows_in.shape), same(grad.shape)]
            + [per_head(shape) for shape in (weights[0].shape[1:],) + shapes] * 2,
            out_specs=[per_head(shape) for shape, _ in results] * 2 + [same(rows_in.shape)],
        ),
        out_shape=[jax.ShapeDtypeStruct((heads,) + shape, kind) for shape, kind in results] * 2
        + [jax.ShapeDtypeStruct((count, width), F32)],
        compiler_params=pltpu.CompilerParams(vmem_limit_bytes=VMEM_BYTES),
        cost_estimate=pl.CostEstimate(
            flops=2 * flops, bytes_accessed=heads * 10 * 2**20, transcendentals=0
        ),
    )(half, rows_in, grad, *[value for part in (0, 1) for value in (weights[part], *saved[part])])
    return (out[:3], out[3:]), rows_grad


def in_order(order, ref):
    return jnp.concatenate([ref[0, order[pl.num_programs(0) + part]] for part in range(4)], axis=0)


def units_forward_kernel(x_ref, g_ref, up_ref, b_ref, hidden_ref, slope_ref, grad_ref):
    weights = up_ref[0].reshape(-1, up_ref.shape[-1])
    value = dot_nt(weights, x_ref[...]) + b_ref[0]
    root, cubic = 0.7978845608028654, 0.044715
    square = value * value
    bent = jnp.tanh(root * value * (1.0 + cubic * square))
    above = 0.5 * (1.0 + bent)
    hidden = low(value * above)
    hidden_ref[0] = hidden.reshape(hidden_ref.shape[1:])
    slope = above + 0.5 * value * (1.0 - bent * bent) * (root * (1.0 + 3.0 * cubic * square))
    slope_ref[0] = low(slope).reshape(slope_ref.shape[1:])
    grad_ref[0] = low(dot_nn(hidden, g_ref[...])).reshape(grad_ref.shape[1:])


def units_backward_kernel(
    order, x_ref, g_ref, up_ref, slope_ref, down_ref, down_other_ref, own_ref, other_ref, b_ref, sum_ref
):
    width = x_ref.shape[1]
    down = jnp.concatenate([ref[0].reshape(-1, width) for ref in (down_ref, down_other_ref)], axis=0)
    grad_pre = low(dot_nt(down, g_ref[...]) * in_order(order, slope_ref).astype(F32))
    b_ref[0] = jnp.sum(grad_pre.astype(F32), axis=1, keepdims=True)
    grad = low(dot_nn(grad_pre, x_ref[...]))
    half = grad.shape[0] // 2
    own_ref[0] = grad[:half].reshape(own_ref.shape[1:])
    other_ref[0] = grad[half:].reshape(own_ref.shape[1:])
    add_up(sum_ref, dot_tn(grad_pre, in_order(order, up_ref)))


def units_out_kernel(order, hidden_ref, down_ref, down_other_ref, sum_ref):
    width = down_ref.shape[-1]
    down = jnp.concatenate([ref[0].reshape(-1, width) for ref in (down_ref, down_other_ref)], axis=0)
    add_up(sum_ref, dot_tn(in_order(order, hidden_ref), down))


def whole(shape):
    return pl.BlockSpec(shape, lambda slot, *order: (0,) * len(shape))


def by_slot(shape):
    return pl.BlockSpec((1,) + shape, lambda slot, *order: (slot,) + (0,) * len(shape))


def by_shard(shape):
    return pl.BlockSpec((1,) + shape, lambda slot, order: (order[slot],) + (0,) * len(shape))


def units_call(kernel, order, slots, inputs, outputs):
    return pl.pallas_call(
        kernel,
        grid_spec=pltpu.PrefetchScalarGridSpec(
            num_scalar_prefetch=len(order),
            grid=(slots,),
            in_specs=[
                kind(value.shape if kind is whole else value.shape[1:]) for kind, value in inputs
            ],
            out_specs=[kind(shape if kind is whole else shape[1:]) for kind, shape, _ in outputs],
        ),
        out_shape=[jax.ShapeDtypeStruct(shape, kept) for _, shape, kept in outputs],
        compiler_params=pltpu.CompilerParams(vmem_limit_bytes=VMEM_BYTES),
        cost_estimate=pl.CostEstimate(
            flops=slots * 4 * 10**8, bytes_accessed=slots * 8 * 2**20, transcendentals=0
        ),
    )(*order, *[value for _, value in inputs])


def window_entries(offset_index):
    side = int(round(offset_index.shape[0] ** 0.5))
    by_place = offset_index.reshape(side, side, side, side)
    rising = by_place[::-1, :, 0, :].transpose(1, 0, 2)
    unused = jnp.full((side, 1, side), -1, offset_index.dtype)
    return jnp.concatenate([rising, by_place[0, :, 1:, :], unused], axis=1)


def windows_kernel(entries_ref, table_ref, out_ref):
    wanted = entries_ref[0]
    place = lax.broadcasted_iota(jnp.int32, (table_ref.shape[1], wanted.shape[1]), 0)
    out_ref[0] = dot_nn(table_ref[...], low(jnp.where(place == wanted, 1.0, 0.0)))


def table_windows(table, entries):
    side = entries.shape[0]
    flat = entries.reshape(side, 1, -1)
    shape = (side, table.shape[0], flat.shape[2])
    (found,) = units_call(
        windows_kernel, (), side, [(by_slot, flat), (whole, table)], [(by_slot, shape, F32)]
    )
    return found.transpose(1, 0, 2)


def table_kernel(entries_ref, windows_ref, sum_ref):
    wanted = entries_ref[0]
    place = lax.broadcasted_iota(jnp.int32, (sum_ref.shape[1], wanted.shape[1]), 0)
    pick = low(jnp.where(place == wanted, 1.0, 0.0))
    rest = windows_ref[0]
    total = jnp.zeros(sum_ref.shape, F32)
    for _ in range(3):
        part = low(rest)
        total += dot_nt(part, pick)
        rest = rest - part.astype(F32)
    add_up(sum_ref, total)


def table_from_windows(windows, entries, table_rows):
    side = entries.shape[0]
    flat = entries.reshape(side, 1, -1)
    (total,) = units_call(
        table_kernel,
        (),
        side,
        [(by_slot, flat), (by_slot, windows.transpose(1, 0, 2))],
        [(whole, (windows.shape[0], table_rows), F32)],
    )
    return total


def normalize(values):
    centred = values - jnp.mean(values, axis=-1, keepdims=True)
    inverse = lax.rsqrt(jnp.mean(centred * centred, axis=-1, keepdims=True) + EPSILON)
    return (centred * inverse, inverse)


def norm_back(grad_normed, normed, inverse):
    first_mean = jnp.mean(grad_normed, axis=-1, keepdims=True)
    second_mean = jnp.mean(grad_normed * normed, axis=-1, keepdims=True)
    return (grad_normed - first_mean - normed * second_mean) * inverse


def attention_rows(qkv_weight, out_weight):
    width, _, local_width = qkv_weight.shape
    heads = local_width // HS
    qkv = qkv_weight.reshape(width, 3, heads, HS).transpose(2, 1, 3, 0)
    out = out_weight.reshape(heads, 1, HS, width)
    return jnp.concatenate([qkv, out], axis=1).reshape(heads * 4 * HS, width)


class Work:
    def __init__(
        self,
        plan,
        tokens,
        conditioning,
        counts,
        offset_index,
        modulator,
        modulator_bias,
        qkv_weight,
        qv_bias,
        offset_table,
        out_weight,
        out_bias,
        up_weight,
        up_bias,
        down_weight,
        down_bias,
        out_grad,
    ):
        self.plan = plan
        self.rows, self.width = tokens.shape
        self.patches = offset_index.shape[0]
        self.samples = self.rows // self.patches
        self.group_samples = conditioning.shape[0]
        self.shards = self.group_samples // self.samples
        self.columns = modulator.shape[1]
        self.local_width = qkv_weight.shape[2]
        self.local_heads = self.local_width // HS
        self.heads = self.local_heads * self.shards
        self.table_rows = offset_table.shape[0]
        self.local_units = up_weight.shape[1]
        self.by_sample = (self.samples, self.patches, self.width)
        self.flat = (self.rows, self.width)
        self.counts, self.offset_index = counts, offset_index
        self.tokens, self.out_grad = tokens, out_grad
        self.conditioning = conditioning.astype(F32)
        self.modulator, self.modulator_bias = modulator, modulator_bias
        self.out_bias, self.down_bias = out_bias, down_bias
        self.attn_rows = attention_rows(qkv_weight, out_weight)
        self.up_rows, self.down_rows = up_weight.T, down_weight
        self.small = jnp.concatenate([qv_bias.reshape(-1), offset_table.T.reshape(-1), up_bias])
        self.half = plan.first_half().reshape(1)
        self.order = plan.unit_order()
        self.attn_w, self.saved = {}, {}
        self.branch = []
        self.up_grads, self.unit_sums, self.grad_input_two_parts = [], [], []
        self.head_grads, self.head_extras, self.rows_grads = {}, {}, []
        self.mlp_parts = []

    def exchange(self, values):
        return lax.all_to_all(values, "mp", 0, 0)

    def to_all(self, values):
        return self.exchange(jnp.broadcast_to(values[None], (self.shards,) + values.shape))

    def modulate(self):
        self.activated = low(jax.nn.silu(self.conditioning))
        part = jnp.dot(self.activated, self.modulator, preferred_element_type=F32)
        part = part + self.modulator_bias.astype(F32)
        mod = self.exchange(part.reshape(self.shards, self.samples, self.columns))
        mod = mod.transpose(1, 0, 2).reshape(self.samples, 6, 1, self.width)
        self.modulation = [mod[:, number] for number in range(6)]

    def norm_one(self):
        shift, scale = self.modulation[:2]
        self.tokens_float = self.tokens.reshape(self.by_sample).astype(F32)
        self.normed_one, self.inverse_one = normalize(self.tokens_float)
        self.input_one = low(self.normed_one * (1.0 + scale) + shift).reshape(self.flat)

    def gather_small(self):
        self.gathered_small = self.to_all(self.small)
        self.all_activated = self.plan.gather_groups(self.activated)

    def prepare(self):
        small, heads = self.gathered_small, self.heads
        cut_one = 2 * self.local_width
        cut_two = cut_one + self.table_rows * self.local_heads
        biases = small[:, :cut_one].reshape(self.shards, 2, self.local_heads, HS).transpose(0, 2, 1, 3)
        biases = biases.reshape(heads, 2, HS).astype(F32)
        self.head_bias = self.plan.to_own(jnp.concatenate([biases, jnp.zeros_like(biases)], axis=2))
        self.entries = window_entries(self.offset_index)
        table = small[:, cut_one:cut_two].reshape(heads, self.table_rows)
        table = self.plan.to_own(table).reshape(heads, self.table_rows)
        windows = table_windows(table, self.entries)
        self.windows = windows.reshape((2, heads // 2) + windows.shape[1:])
        self.up_biases = small[:, cut_two:].astype(F32)[:, :, None]

    def forward_weights(self, number, own, other):
        self.attn_w[number] = (own, other)

    def forward(self, number):
        self.saved[number], branch = attention_forward(
            self.half,
            self.input_one,
            self.attn_w[number],
            [self.plan.chunk(number, part) for part in self.head_bias],
            [self.plan.chunk(number, part) for part in self.windows],
            self.patches,
        )
        self.branch = self.branch + [branch]

    def norm_two(self):
        _, _, gate_one, shift, scale, gate_two = self.modulation
        first = lax.axis_index("mp") * self.samples
        live = first + jnp.arange(self.samples, dtype=jnp.int32) < self.counts[0]
        self.live = live.astype(F32)[:, None, None]
        self.attn_branch = sum(self.branch).reshape(self.by_sample) + self.out_bias.astype(F32)
        self.mid = self.tokens_float + gate_one * self.attn_branch
        self.normed_two, self.inverse_two = normalize(self.mid)
        self.input_two = low(self.normed_two * (1.0 + scale) + shift).reshape(self.flat)
        self.grad_final = self.out_grad.reshape(self.by_sample).astype(F32) * self.live
        self.mlp_grad = low(gate_two * self.grad_final).reshape(self.flat)

    def units_forward(self):
        quarter = self.local_units // 4
        weights = (self.shards, 4, quarter, self.width)
        values = (self.shards, 4, quarter, self.rows)
        self.up_w = self.up_w.reshape(weights)
        self.hidden, self.slope, self.down_grad = units_call(
            units_forward_kernel,
            (),
            self.shards,
            [
                (whole, self.input_two),
                (whole, self.mlp_grad),
                (by_slot, self.up_w),
                (by_slot, self.up_biases),
            ],
            [(by_slot, values, BF16), (by_slot, values, BF16), (by_slot, weights, BF16)],
        )
        self.units_in = (self.input_two, self.mlp_grad)

    def part_order(self, part):
        shards, quarters = self.order
        slots = self.shards // 2
        return slots, (jnp.concatenate([shards[part * slots : (part + 1) * slots], quarters]),)

    def units_backward(self, part):
        slots, order = self.part_order(part)
        piece = (slots, 2, self.local_units // 4, self.width)
        own, other, sums, grad = units_call(
            units_backward_kernel,
            order,
            slots,
            [
                (whole, self.units_in[0]),
                (whole, self.units_in[1]),
                (by_shard, self.up_w),
                (by_shard, self.slope),
                (by_slot, self.down_w[part][0]),
                (by_slot, self.down_w[part][1]),
            ],
            [
                (by_slot, piece, BF16),
                (by_slot, piece, BF16),
                (by_slot, (slots, self.local_units, 1), F32),
                (whole, self.flat, F32),
            ],
        )
        self.up_grads = self.up_grads + [(own, other)]
        self.unit_sums = self.unit_sums + [sums]
        self.grad_input_two_parts = self.grad_input_two_parts + [grad]

    def norm_two_back(self):
        _, _, gate_one, _, scale, _ = self.modulation
        self.grad_input_two = sum(self.grad_input_two_parts).reshape(self.by_sample)
        grad_normed = self.grad_input_two * (1.0 + scale)
        self.grad_mid = self.grad_final + norm_back(grad_normed, self.normed_two, self.inverse_two)
        self.attn_grad = low(gate_one * self.grad_mid).reshape(self.flat)

    def backward(self, number):
        sides, rows_grad = attention_backward(
            self.half,
            self.input_one,
            self.attn_grad,
            self.attn_w[number],
            self.saved[number],
            self.windows.shape[2:],
            self.patches,
        )
        self.head_grads = {**self.head_grads, number: tuple(side[0] for side in sides)}
        self.head_extras[number] = [side[1:] for side in sides]
        self.rows_grads = self.rows_grads + [rows_grad]

    def units_out(self):
        self.mlp_parts = []
        for part in (0, 1):
            slots, order = self.part_order(part)
            self.mlp_parts += units_call(
                units_out_kernel,
                order,
                slots,
                [
                    (by_shard, self.hidden),
                    (by_slot, self.down_w[part][0]),
                    (by_slot, self.down_w[part][1]),
                ],
                [(whole, self.flat, F32)],
            )

    def finish_rows(self):
        _, scale_one, _, _, _, gate_two = self.modulation
        mlp_branch = sum(self.mlp_parts).reshape(self.by_sample) + self.down_bias.astype(F32)
        self.block_out = low((self.mid + gate_two * mlp_branch) * self.live).reshape(self.flat)
        grad_input_one = sum(self.rows_grads).reshape(self.by_sample)
        grad_normed = grad_input_one * (1.0 + scale_one)
        tokens_grad = self.grad_mid + norm_back(grad_normed, self.normed_one, self.inverse_one)
        self.tokens_grad = tokens_grad.reshape(self.flat)
        terms = (
            grad_input_one,
            grad_input_one * self.normed_one,
            self.grad_mid * self.attn_branch,
            self.grad_input_two,
            self.grad_input_two * self.normed_two,
            self.grad_final * mlp_branch,
        )
        mod_grad = low(jnp.stack([jnp.sum(term, axis=1) for term in terms], axis=1))
        mod_grad = mod_grad.reshape(self.samples, self.shards, self.columns)
        self.mod_grad = mod_grad.transpose(1, 0, 2)
        self.sums = jnp.stack(
            [jnp.sum(part.astype(F32), axis=0) for part in (self.attn_grad, self.mlp_grad)]
        )

    def extras(self, place):
        numbers = range(len(self.head_extras))
        sides = [[self.head_extras[number][side][place] for number in numbers] for side in (0, 1)]
        return self.plan.to_whole(jnp.stack([self.plan.in_slots(side) for side in sides]))

    def finish_small(self):
        shards, columns = self.shards, self.columns
        head_grads = self.extras(0)[:, :, :HS].reshape(shards, -1)
        table_grads = table_from_windows(self.extras(1), self.entries, self.table_rows).reshape(shards, -1)
        unit_grads = self.plan.units_to_whole(jnp.concatenate(self.unit_sums)).reshape(shards, -1)
        parts = [head_grads, table_grads, unit_grads, self.sums.reshape(shards, -1)]
        sizes = [part.shape[1] for part in parts]
        parts.append(self.mod_grad.reshape(shards, -1).astype(F32))
        came = self.exchange(jnp.concatenate(parts, axis=1))
        total_size = sum(sizes)
        mod_grad = low(came[:, total_size:]).reshape(self.group_samples, columns)
        act_grad = low(dot_nt(mod_grad, self.modulator)).reshape(shards, self.samples, self.width)
        act_grad = jnp.sum(self.exchange(act_grad).astype(F32), axis=0)
        totals = jnp.sum(came[:, :total_size], axis=0)
        totals = self.plan.sum_groups(totals)
        all_mod_grad = self.plan.gather_groups(mod_grad)
        self.modulator_grad = dot_tn(self.all_activated, all_mod_grad)
        self.modulator_bias_grad = jnp.sum(all_mod_grad.astype(F32), axis=0)
        cuts = [sum(sizes[:number]) for number in (1, 2, 3)]
        head_part, table_part, self.up_bias_grad, row_part = jnp.split(totals, cuts)
        head_part = head_part.reshape(self.local_heads, 2, HS).transpose(1, 0, 2)
        self.qv_bias_grad = head_part.reshape(2, self.local_width)
        self.offset_table_grad = table_part.reshape(self.local_heads, self.table_rows).T
        last = self.to_all(jnp.concatenate([act_grad.reshape(-1), row_part]))
        cut = act_grad.size
        act_grad = low(last[:, :cut]).astype(F32).reshape(self.group_samples, self.width)
        self.out_bias_grad, self.down_bias_grad = last[:, cut:].reshape(2, self.width)
        _, silu_back = jax.vjp(jax.nn.silu, self.conditioning)
        self.cond_grad = silu_back(act_grad)[0]

    def outputs(self):
        attn = self.attn_shard.reshape(self.local_heads, 4, HS, self.width)
        qkv_grad = attn[:, :3].transpose(3, 1, 0, 2).reshape(self.width, 3, self.local_width)
        return (
            self.block_out,
            self.tokens_grad,
            self.cond_grad,
            self.modulator_grad,
            self.modulator_bias_grad,
            qkv_grad,
            self.qv_bias_grad,
            self.offset_table_grad,
            attn[:, 3].reshape(self.local_width, self.width),
            self.out_bias_grad,
            self.up_shard.T,
            self.up_bias_grad,
            self.down_shard,
            self.down_bias_grad,
        )


def local(plan, *arguments):
    work = Work(plan, *arguments)
    plan.run(work)
    return work.outputs()


def solution(mesh):
    known = (mesh.shape["dp"], mesh.shape["mp"]) == (4, 8)
    plan = PairPlan(mesh) if known else PlainPlan(mesh)
    in_specs = (
        P(("dp", "mp"), None),
        P("dp", None),
        P("dp"),
        P(),
        P(None, "mp"),
        P("mp"),
        P(None, None, "mp"),
        P(None, "mp"),
        P(None, "mp"),
        P("mp", None),
        P(),
        P(None, "mp"),
        P("mp"),
        P("mp", None),
        P(),
        P(("dp", "mp"), None),
    )
    out_specs = (
        P(("dp", "mp"), None),
        P(("dp", "mp"), None),
        P("dp", None),
        P(None, "mp"),
        P("mp"),
        P(None, None, "mp"),
        P(None, "mp"),
        P(None, "mp"),
        P("mp", None),
        P(),
        P(None, "mp"),
        P("mp"),
        P("mp", None),
        P(),
    )
    return jax.shard_map(
        partial(local, plan), mesh=mesh, in_specs=in_specs, out_specs=out_specs, check_vma=False
    )
```
